32 devices in a mesh: lat: 4 (over x, core), lon: 8 (over z, y).
Axes of the slice: x: 2, y: 2, z: 4, core: 2. Of those that a mesh axis runs over, the one named last changes fastest.
Arguments:
- control: float32 [16, 256, 8192], P(None, 'lat', 'lon'), may hold values from -6 to 6
- sigma_field: float32 [16, 256, 8192], P(None, 'lat', 'lon'), may hold values from 0.3 to 3
- mixing: float32 [16, 16], replicated, may hold values from -1.5 to 1.5
- zonal_reach: int32 [256], P('lat'), may hold values from 1 to 64, as said below
- obs_owner: int32 [65536, 1], P(('lat', 'lon')), may hold values from 0 to 31; in each aligned block of 2048 rows (0 to 2047, 2048 to 4095, ...) at most 64 rows name the same one
- obs_cell: int32 [65536], P(('lat', 'lon')), may hold values from 0 to 65535
- obs_chan: int32 [65536], P(('lat', 'lon')), may hold values from 0 to 15
- obs_weight: bfloat16 [65536], P(('lat', 'lon')), may hold values from -48 to 48
Outputs:
- increment: float32 [16, 256, 8192], P(None, 'lat', 'lon')
- gradient: float32 [16, 256, 8192], P(None, 'lat', 'lon')
The draws below stay inside these ranges and needn't reach their ends.
Inputs may be any that keep to these rules, and one draw needn't show every extreme that they name: `zonal_reach`: rows next to either pole have reach 64. `obs_owner`: devices are numbered in the order of the joined axis lat+lon; among the observations held by one device at most 64 name the same owner.
All inputs are finite; a program needn't handle non-finite values.
Results may differ from the reference program's by a relative error of at most 0.0003.
Values may be sent and summed in bfloat16 or wider, within the bound.
A program may use at most 128 MiB of HBM per device.

```python
import math
import jax
import jax.numpy as jnp
import numpy as np
from jax import lax

C = 16
ROWS_DEV = 64
COLS_DEV = 1024
OBS_DEV = 2048
CAP = 64
MAXREACH = 64
MREACH = 8
NLAT = 256
NLON = 8192
NOBS = 65536
N_LON = 8
DEVICES = 32


def draw_zonal_reach(key, part):
    row_ids = jnp.arange(NLAT, dtype=jnp.int32)
    pole_distance = jnp.minimum(row_ids, NLAT - 1 - row_ids)
    lowest = jnp.maximum(1, MAXREACH - pole_distance * (4 * MAXREACH) // NLAT)
    return jax.random.randint(key, (NLAT,), lowest, MAXREACH + 1, dtype=jnp.int32)


def set_ends(values, key, low, largest):
    spot = [jax.random.randint(jax.random.fold_in(key, axis), (), 0, length) for axis, length in enumerate(values.shape)]
    main_axis = values.shape.index(max(values.shape))
    next_to = spot[:main_axis] + [(spot[main_axis] + 1) % values.shape[main_axis]] + spot[main_axis + 1:]
    return values.at[tuple(spot)].set(low).at[tuple(next_to)].set(largest)


def level_of(stream_key, dims, pieces, low, high):
    gain, own = 1.0, jax.random.fold_in(stream_key, 6)
    for dim, parts in pieces:
        heights = jnp.exp(jax.random.uniform(jax.random.fold_in(own, dim), (parts,), jnp.float32, low / len(pieces), high / len(pieces)))
        gain = gain * jnp.repeat(heights, dims[dim] // parts).reshape([-1 if axis == dim else 1 for axis in range(len(dims))])
    return gain


def assign_block(stream_key, own, number, rows, count, top, most, lean):
    order = jax.random.permutation(stream_key, count)
    crowded, common = load_shares(count, rows * top, most, lean, True), load_shares(count, rows * top, most, lean, False)
    places = jnp.arange(count)

    def named(sizes, turn):
        used = int((sizes > 0).sum())
        fixed = max(1, used // 4)
        moved = fixed + (places - fixed + turn * (used - fixed)) % max(1, count - fixed)
        return jnp.zeros((count,), jnp.int32).at[order[jnp.where(places < fixed, places, moved)]].set(jnp.asarray(sizes, jnp.int32))

    sizes = jnp.where(number % 4 == 0, named(crowded, number // 4), named(common, number - number // 4 - 1))
    mixed = jax.random.permutation(jax.random.fold_in(own, 3), count)
    source_of, sink = mixed[0:count // 2 * 2:2], mixed[1:count // 2 * 2:2]
    margin = jnp.minimum(sizes[source_of] - 1, most - sizes[sink]) // 2
    margin = jnp.where((source_of == order[0]) | (sink == order[0]) | (sizes[sink] == 0), 0, jnp.maximum(margin, 0))
    moved = jax.random.randint(jax.random.fold_in(own, 4), (count // 2,), 0, 1 << 20) % (margin + 1)
    sizes = sizes.at[source_of].add(-moved).at[sink].add(moved)
    labels = jnp.searchsorted(jnp.cumsum(sizes), jnp.arange(rows * top), side="right").astype(jnp.int32)
    grid = labels.reshape(top, rows).T
    grid = grid[jax.random.permutation(jax.random.fold_in(own, 1), rows)]
    turn = jax.random.randint(jax.random.fold_in(own, 2), (rows, 1), 0, top)
    return jnp.take_along_axis(grid, (jnp.arange(top)[None, :] + turn) % top, axis=1)


def load_shares(amount, total, reach, lean, full):
    portions = [(1 << 20) // math.isqrt(standing ** lean) + 1 for standing in range(1, amount + 1)]
    largest = reach if full else min(reach, max(-(-total // amount), total * portions[0] // sum(portions)))
    least = 1 if total - largest >= amount - 1 else 0
    holding, surplus = [largest] + [least] * (amount - 1), total - largest - least * (amount - 1)
    while surplus > 0:
        movable = [i for i in range(1, amount) if holding[i] < largest] or [i for i in range(1, amount) if holding[i] < reach]
        whole, left = sum([portions[i] for i in movable]), surplus
        for i in movable:
            extra = min(reach - holding[i], max(1, left * portions[i] // whole), surplus)
            holding[i] = holding[i] + extra
            surplus = surplus - extra
    return np.array(holding)


def normal_values(rng, dims, deviation, limit, pieces=(), kind=jnp.bfloat16):
    drawn = deviation * jax.random.normal(rng, dims, jnp.float32)
    if pieces:
        drawn = drawn * level_of(rng, dims, pieces, -0.22, 0.18)
    return jnp.clip(drawn, -limit, limit).astype(kind)


def setup_inputs(seed: int = 0) -> dict:
    arg_keys = jax.random.split(jax.random.key(seed), 9)
    control = normal_values(arg_keys[0], (C, NLAT, NLON), 1.0, 6.0, ((1, 4), (2, 8)), jnp.float32)
    sigma_field = jnp.clip(jnp.exp(math.log(3.0) - 2.3025851 * jax.random.uniform(arg_keys[1], (C, NLAT, NLON), jnp.float32) ** level_of(arg_keys[1], (C, NLAT, NLON), ((1, 4), (2, 8)), -0.2, 0.2)), 0.3, 3.0)
    mixing = normal_values(arg_keys[2], (C, C), C ** -0.5, 1.5, (), jnp.float32)
    zonal_reach = draw_zonal_reach(jax.random.fold_in(arg_keys[8], 71), 0)
    obs_owner_keys = jax.random.split(jax.random.fold_in(arg_keys[4], 1), NOBS // OBS_DEV)
    obs_owner_turns = jax.random.permutation(jax.random.fold_in(arg_keys[4], 3), NOBS // OBS_DEV)
    obs_owner = jax.vmap(lambda own, number: assign_block(jax.random.fold_in(arg_keys[4], 2), own, number, OBS_DEV, DEVICES, 1, CAP, 2))(obs_owner_keys, obs_owner_turns).reshape((NOBS, 1))
    obs_cell = set_ends(jax.random.randint(arg_keys[5], (NOBS,), 0, ROWS_DEV * COLS_DEV), jax.random.fold_in(arg_keys[5], 1), 0, (ROWS_DEV * COLS_DEV) - 1).astype(jnp.int32)
    obs_chan = set_ends(jax.random.randint(arg_keys[6], (NOBS,), 0, C), jax.random.fold_in(arg_keys[6], 1), 0, C - 1).astype(jnp.int32)
    obs_weight = normal_values(arg_keys[7], (NOBS,), 8.0, 48.0, ((0, 32),))
    return dict(control=control, sigma_field=sigma_field, mixing=mixing, zonal_reach=zonal_reach, obs_owner=obs_owner, obs_cell=obs_cell, obs_chan=obs_chan, obs_weight=obs_weight)


def kernel_weights(offsets, reach_cells):
    scaled = 3.0 * offsets / reach_cells
    return jnp.where(jnp.abs(offsets) <= reach_cells, jnp.exp(-0.5 * scaled * scaled), jnp.zeros_like(scaled))

def zonal_smooth(field, zonal_reach):
    offsets = jnp.arange(-MAXREACH, MAXREACH + 1).astype(jnp.float32)
    reach_cells = zonal_reach.astype(jnp.float32)[:, None]
    tap_table = kernel_weights(offsets[None, :], reach_cells)
    tap_table = tap_table / jnp.sqrt(lax.optimization_barrier(jnp.sum(tap_table * tap_table, axis=1, keepdims=True)))

    def add_offset(offset_id, running):
        weights = lax.dynamic_index_in_dim(tap_table, offset_id, 1, keepdims=False)
        rolled = jnp.roll(field, MAXREACH - offset_id, axis=2)
        return running + weights[None, :, None] * rolled
    return lax.fori_loop(0, 2 * MAXREACH + 1, add_offset, jnp.zeros_like(field))

def meridional(field):
    offsets = jnp.arange(-MREACH, MREACH + 1).astype(jnp.float32)
    merid_taps = kernel_weights(offsets, jnp.float32(MREACH))
    merid_taps = merid_taps / jnp.sqrt(jnp.sum(merid_taps * merid_taps))
    padded = jnp.pad(field, ((0, 0), (MREACH, MREACH), (0, 0)))

    def add_offset(offset_id, running):
        piece = lax.dynamic_slice_in_dim(padded, offset_id, field.shape[1], 1)
        return running + merid_taps[offset_id] * piece
    return lax.fori_loop(0, 2 * MREACH + 1, add_offset, jnp.zeros_like(field))

def reference(control, sigma_field, mixing, zonal_reach, obs_owner, obs_cell, obs_chan, obs_weight):
    mixed_field = jnp.einsum('cd,dij->cij', mixing, control, precision=lax.Precision.HIGHEST)
    increment = sigma_field * zonal_smooth(meridional(mixed_field), zonal_reach)
    owner_ids = obs_owner[:, 0]
    global_row = owner_ids // N_LON * ROWS_DEV + obs_cell // COLS_DEV
    global_col = owner_ids % N_LON * COLS_DEV + obs_cell % COLS_DEV
    scattered = jnp.zeros((C, NLAT, NLON), jnp.float32).at[obs_chan, global_row, global_col].add(obs_weight.astype(jnp.float32))
    merid_adj = meridional(zonal_smooth(sigma_field * scattered, zonal_reach))
    gradient = jnp.einsum('dc,dij->cij', mixing, merid_adj, precision=lax.Precision.HIGHEST)
    return (increment, gradient)
```

```python
import math

import jax
import jax.numpy as jnp
from jax import lax
from jax.experimental import pallas as pl
from jax.experimental.pallas import tpu as pltpu
from jax.sharding import PartitionSpec as P

CAP = 64
MAXREACH = 64
MREACH = 8
GROUP = 16
TILE = 128
BF = jnp.bfloat16
F32 = jnp.float32
LOG2E = math.log2(math.e)


def merid_weights(lag):
    taps = [math.exp(-0.5 * (3.0 * t / MREACH) ** 2) for t in range(-MREACH, MREACH + 1)]
    norm = math.sqrt(sum(w * w for w in taps))
    scaled = lag * (3.0 / MREACH)
    return jnp.where(jnp.abs(lag) <= MREACH, jnp.exp(-0.5 * scaled * scaled) / norm, 0.0)


def kron_matrices(mixing):
    channels = mixing.shape[0]
    a = jnp.arange(GROUP)[:, None]
    p = jnp.arange(2 * GROUP)[None, :]
    band = merid_weights((p - a - MREACH).astype(F32)).reshape(GROUP, 2, GROUP)
    size = GROUP * channels
    fwd = band.transpose(1, 0, 2)[:, :, None, None, :] * mixing[None, None, :, :, None]
    fwd = fwd.reshape(2, size, size)
    adj = band.transpose(1, 0, 2)[:, None, :, :, None] * mixing.T[None, :, None, None, :]
    adj = adj.reshape(2, size, size)
    return fwd, adj


def row_params(zonal_reach):
    reach = zonal_reach.astype(F32)
    t = jnp.arange(-MAXREACH, MAXREACH + 1).astype(F32)
    scaled = 3.0 * t[None, :] / reach[:, None]
    taps = jnp.where(jnp.abs(t)[None, :] <= reach[:, None], jnp.exp(-0.5 * scaled * scaled), 0.0)
    log_norm = -0.5 * jnp.log2(jnp.sum(taps * taps, axis=1))
    return jnp.stack([-4.5 * LOG2E / (reach * reach), log_norm, reach * reach])


def split(x):
    hi = x.astype(BF)
    return hi, (x - hi.astype(F32)).astype(BF)


def dot(a, b):
    return jnp.dot(a, b, preferred_element_type=F32)


def lag_squared():
    p = lax.broadcasted_iota(jnp.int32, (2 * TILE, TILE), 0)
    j = lax.broadcasted_iota(jnp.int32, (2 * TILE, TILE), 1)
    lag = (p - j - MAXREACH).astype(F32)
    return lag * lag


def zonal_rows(hi_ref, lo_ref, out_ref, params_ref, first_row, blocks):
    t2 = lag_squared()
    channels = hi_ref.shape[0] // GROUP
    for r in range(GROUP):
        row = first_row + r
        coef, shift, limit = params_ref[0, row], params_ref[1, row], params_ref[2, row]
        band = jnp.where(t2 <= limit, jnp.exp2(t2 * coef + shift), 0.0)
        band = jnp.concatenate(split(band), axis=1)
        rows = slice(r * channels, (r + 1) * channels)
        parts = []
        for ref in (hi_ref, lo_ref):
            for b in range(blocks):
                parts.append(ref[rows, b * TILE:(b + 2) * TILE])
        prod = dot(jnp.concatenate(parts, axis=0), band)
        n = blocks * channels
        total = prod[:n, :TILE] + (prod[:n, TILE:] + prod[n:, :TILE])
        for b in range(blocks):
            out_ref[rows, b * TILE:(b + 1) * TILE] = total[b * channels:(b + 1) * channels]


def prep_kernel(devices, owner_ref, cell_ref, chan_ref, weight_ref, out_ref):
    count = owner_ref.shape[1]
    chunk = math.gcd(count, 256)
    owner = owner_ref[...]
    hits = lax.broadcasted_iota(jnp.int32, (devices, count), 0) == owner
    hits_f = jnp.where(hits, 1.0, 0.0)
    hits_b = hits_f.astype(BF)
    upper = (
        lax.broadcasted_iota(jnp.int32, (chunk, chunk), 0)
        < lax.broadcasted_iota(jnp.int32, (chunk, chunk), 1)
    )
    upper = jnp.where(upper, 1.0, 0.0).astype(BF)
    base = jnp.zeros((devices, 1), F32)
    ranks = []
    for k in range(count // chunk):
        cols = slice(k * chunk, (k + 1) * chunk)
        before = dot(hits_b[:, cols], upper) + base
        ranks.append(jnp.sum(before * hits_f[:, cols], axis=0, keepdims=True))
        base = base + jnp.sum(hits_f[:, cols], axis=1, keepdims=True)
    rank = jnp.concatenate(ranks, axis=1).astype(jnp.int32)
    rank_hits = lax.broadcasted_iota(jnp.int32, (CAP, count), 0) == rank
    flat = cell_ref[...] + chan_ref[...]
    digits = [flat & 127, (flat >> 7) & 127, flat >> 14]
    pieces = [weight_ref[...].astype(F32)] + [d.astype(F32) for d in digits]
    table = jnp.concatenate([jnp.where(rank_hits, v, 0.0) for v in pieces], axis=0).astype(BF)
    out = lax.dot_general(hits_b, table, (((1,), (1,)), ((), ())), preferred_element_type=F32)
    out_ref[...] = out.astype(BF)


def adjoint_kernel(
    params_ref, got_ref, sigma_ref, kron_ref, out_ref,
    colhot, work, hi_ref, lo_ref, zon_ref, carry, kron_hi, kron_lo,
):
    step = pl.program_id(0)
    groups = pl.num_programs(0) - 1
    channels, _, cols = sigma_ref.shape
    received = got_ref.shape[1]
    lines = channels * GROUP
    wide = cols + TILE
    chunk = math.gcd(received, 2048)

    def place(k):
        digits = got_ref[:, k * chunk:(k + 1) * chunk].astype(F32)
        flat = digits[1:2] + 128.0 * digits[2:3] + 16384.0 * digits[3:4]
        return digits[0:1], flat.astype(jnp.int32)

    @pl.when(step == 0)
    def _():
        hi, lo = split(kron_ref[...])
        kron_hi[...] = hi
        kron_lo[...] = lo
        carry[...] = jnp.zeros_like(carry)
        hi_ref[...] = jnp.zeros_like(hi_ref)
        lo_ref[...] = jnp.zeros_like(lo_ref)
        for k in range(received // chunk):
            col = place(k)[1] % cols
            hot = lax.broadcasted_iota(jnp.int32, (cols, chunk), 0) == col
            colhot[:, k * chunk:(k + 1) * chunk] = jnp.where(hot, 1.0, 0.0).astype(BF)

    @pl.when(step < groups)
    def _():
        place_ids = lax.broadcasted_iota(jnp.int32, (lines, chunk), 0)
        total = jnp.zeros((lines, cols), F32)
        for k in range(received // chunk):
            value, flat = place(k)
            line = flat // cols
            chan, row = line % channels, line // channels - step * GROUP
            inside = (row >= 0) & (row < GROUP)
            target = jnp.where(inside, chan * GROUP + row, -1)
            rowhot = jnp.where(place_ids == target, value, 0.0).astype(BF)
            total = total + lax.dot_general(
                rowhot, colhot[:, k * chunk:(k + 1) * chunk],
                (((1,), (1,)), ((), ())), preferred_element_type=F32,
            )
        weighted = total.reshape(channels, GROUP, cols) * sigma_ref[...]
        weighted = jnp.swapaxes(weighted, 0, 1).reshape(lines, cols)
        hi, lo = split(weighted)
        hi_ref[:, TILE:TILE + cols] = hi
        lo_ref[:, TILE:TILE + cols] = lo
        zonal_rows(hi_ref, lo_ref, zon_ref, params_ref, step * GROUP, wide // TILE)
        z_hi, z_lo = split(zon_ref[...])
        done = carry[...] + (
            dot(kron_hi[1], z_hi) + (dot(kron_hi[1], z_lo) + dot(kron_lo[1], z_hi))
        )
        out_ref[...] = done.reshape(channels, GROUP, wide)
        carry[...] = dot(kron_hi[0], z_hi) + (dot(kron_hi[0], z_lo) + dot(kron_lo[0], z_hi))

    @pl.when(step == groups)
    def _():
        out_ref[...] = carry[...].reshape(channels, GROUP, wide)


def forward_kernel(
    params_ref, low_ref, high_ref, sigma_ref, kron_ref, out_ref,
    hi_ref, lo_ref, zon_ref, kron_hi, kron_lo,
):
    step = pl.program_id(0)
    channels, _, cols = sigma_ref.shape
    lines = channels * GROUP
    wide = cols + TILE

    @pl.when(step == 0)
    def _():
        hi, lo = split(kron_ref[...])
        kron_hi[...] = hi
        kron_lo[...] = lo

    total = None
    for half, ref in enumerate((low_ref, high_ref)):
        hi, lo = split(ref[...].reshape(lines, wide))
        part = dot(kron_hi[half], hi) + (dot(kron_hi[half], lo) + dot(kron_lo[half], hi))
        total = part if total is None else total + part
    hi, lo = split(total)
    hi_ref[...] = hi
    lo_ref[...] = lo
    zonal_rows(hi_ref, lo_ref, zon_ref, params_ref, step * GROUP, cols // TILE)
    smooth = jnp.swapaxes(zon_ref[...].reshape(GROUP, channels, cols), 0, 1)
    out_ref[...] = smooth * sigma_ref[...]


def shifts(axis, periodic):
    count = lax.axis_size(axis)
    forward = [(i, i + 1) for i in range(count - 1)]
    if periodic:
        forward.append((count - 1, 0))
    return forward, [(t, s) for s, t in forward]


def local(control, sigma_field, mixing, zonal_reach, obs_owner, obs_cell, obs_chan, obs_weight):
    channels, rows, cols = control.shape
    devices = lax.axis_size("lat") * lax.axis_size("lon")
    lines, wide, groups = channels * GROUP, cols + TILE, rows // GROUP
    lat_fwd, lat_bwd = shifts("lat", False)
    lon_fwd, lon_bwd = shifts("lon", True)

    low = lax.ppermute(control[:, rows - MREACH:, :], "lat", lat_fwd)
    high = lax.ppermute(control[:, :MREACH, :], "lat", lat_bwd)

    count = obs_cell.shape[0]
    owner = obs_owner.reshape(1, count)
    row, col = obs_cell // cols, obs_cell % cols
    sent = pl.pallas_call(
        lambda *refs: prep_kernel(devices, *refs),
        out_shape=jax.ShapeDtypeStruct((devices, 4 * CAP), BF),
        compiler_params=pltpu.CompilerParams(vmem_limit_bytes=48 * 2**20),
        name="prep",
    )(
        owner,
        (row * (channels * cols) + col).reshape(1, count),
        (obs_chan * cols).reshape(1, count),
        obs_weight.reshape(1, count),
    )
    got = lax.all_to_all(sent, ("lat", "lon"), split_axis=0, concat_axis=0, tiled=True)
    received = devices * CAP
    got = got.reshape(devices, 4, CAP).transpose(1, 0, 2).reshape(4, received)

    params = row_params(zonal_reach)
    kron_fwd, kron_adj = kron_matrices(mixing)

    tall = jnp.concatenate([low, control, high], axis=1)
    left = lax.ppermute(tall[:, :, cols - MAXREACH:], "lon", lon_fwd)
    right = lax.ppermute(tall[:, :, :MAXREACH], "lon", lon_bwd)
    padded = jnp.concatenate([left, tall, right], axis=2)

    smem = pl.BlockSpec(memory_space=pltpu.SMEM)
    vmem = pl.BlockSpec(memory_space=pltpu.VMEM)
    ext = pl.pallas_call(
        adjoint_kernel,
        grid=(groups + 1,),
        in_specs=[
            smem,
            vmem,
            pl.BlockSpec((channels, GROUP, cols), lambda g: (0, jnp.minimum(g, groups - 1), 0)),
            vmem,
        ],
        out_specs=pl.BlockSpec((channels, GROUP, wide), lambda g: (0, g, 0)),
        out_shape=jax.ShapeDtypeStruct((channels, rows + GROUP, wide), F32),
        scratch_shapes=[
            pltpu.VMEM((cols, received), BF),
            pltpu.VMEM((lines, cols), F32),
            pltpu.VMEM((lines, wide + TILE), BF),
            pltpu.VMEM((lines, wide + TILE), BF),
            pltpu.VMEM((lines, wide), F32),
            pltpu.VMEM((lines, wide), F32),
            pltpu.VMEM((2, lines, lines), BF),
            pltpu.VMEM((2, lines, lines), BF),
        ],
        compiler_params=pltpu.CompilerParams(vmem_limit_bytes=52 * 2**20),
        cost_estimate=pl.CostEstimate(
            flops=16 * 10**9, bytes_accessed=10 * 2**20, transcendentals=0
        ),
        name="adjoint",
    )(params, got, sigma_field, kron_adj)

    to_left = lax.ppermute(ext[:, :, :MAXREACH], "lon", lon_bwd)
    to_right = lax.ppermute(ext[:, :, cols + MAXREACH:], "lon", lon_fwd)

    increment = pl.pallas_call(
        forward_kernel,
        grid=(groups,),
        in_specs=[
            smem,
            pl.BlockSpec((channels, GROUP, wide), lambda g: (0, g, 0)),
            pl.BlockSpec((channels, GROUP, wide), lambda g: (0, g + 1, 0)),
            pl.BlockSpec((channels, GROUP, cols), lambda g: (0, g, 0)),
            vmem,
        ],
        out_specs=pl.BlockSpec((channels, GROUP, cols), lambda g: (0, g, 0)),
        out_shape=jax.ShapeDtypeStruct((channels, rows, cols), F32),
        scratch_shapes=[
            pltpu.VMEM((lines, wide), BF),
            pltpu.VMEM((lines, wide), BF),
            pltpu.VMEM((lines, cols), F32),
            pltpu.VMEM((2, lines, lines), BF),
            pltpu.VMEM((2, lines, lines), BF),
        ],
        compiler_params=pltpu.CompilerParams(vmem_limit_bytes=48 * 2**20),
        cost_estimate=pl.CostEstimate(
            flops=12 * 10**9, bytes_accessed=20 * 2**20, transcendentals=0
        ),
        name="forward",
    )(params, padded, padded, sigma_field, kron_fwd)

    inner = ext[:, :, MAXREACH:MAXREACH + cols]
    inner = inner + jnp.pad(to_right, ((0, 0), (0, 0), (0, cols - MAXREACH)))
    inner = inner + jnp.pad(to_left, ((0, 0), (0, 0), (cols - MAXREACH, 0)))
    to_up = lax.ppermute(inner[:, :MREACH], "lat", lat_bwd)
    to_down = lax.ppermute(inner[:, rows + MREACH:], "lat", lat_fwd)
    gradient = inner[:, MREACH:MREACH + rows]
    gradient = gradient + jnp.pad(to_down, ((0, 0), (0, rows - MREACH), (0, 0)))
    gradient = gradient + jnp.pad(to_up, ((0, 0), (rows - MREACH, 0), (0, 0)))
    return (increment, gradient)


def solution(mesh):
    return jax.shard_map(
        local,
        mesh=mesh,
        in_specs=(
            P(None, "lat", "lon"),
            P(None, "lat", "lon"),
            P(),
            P("lat"),
            P(("lat", "lon"), None),
            P(("lat", "lon")),
            P(("lat", "lon")),
            P(("lat", "lon")),
        ),
        out_specs=(P(None, "lat", "lon"), P(None, "lat", "lon")),
        check_vma=False,
    )
```

```python
import functools
import math

import jax
import jax.numpy as jnp
from jax import lax
from jax.experimental import pallas as pl
from jax.experimental.pallas import tpu as pltpu
from jax.sharding import PartitionSpec as P

CAP = 64
MAXREACH = 64
MREACH = 8
GROUP = 16
TILE = 128
BF = jnp.bfloat16
F32 = jnp.float32
LOG2E = math.log2(math.e)


def merid_weights(lag):
    taps = [math.exp(-0.5 * (3.0 * t / MREACH) ** 2) for t in range(-MREACH, MREACH + 1)]
    norm = math.sqrt(sum(w * w for w in taps))
    scaled = lag * (3.0 / MREACH)
    return jnp.where(jnp.abs(lag) <= MREACH, jnp.exp(-0.5 * scaled * scaled) / norm, 0.0)


def row_params(zonal_reach):
    reach = zonal_reach.astype(F32)
    t = jnp.arange(-MAXREACH, MAXREACH + 1).astype(F32)
    scaled = 3.0 * t[None, :] / reach[:, None]
    taps = jnp.where(jnp.abs(t)[None, :] <= reach[:, None], jnp.exp(-0.5 * scaled * scaled), 0.0)
    log_norm = -0.5 * jnp.log2(jnp.sum(taps * taps, axis=1))
    return jnp.stack([-4.5 * LOG2E / (reach * reach), log_norm, reach * reach])


def split(x):
    hi = x.astype(BF)
    return hi, (x - hi.astype(F32)).astype(BF)


def dot(a, b):
    return jnp.dot(a, b, preferred_element_type=F32)


def lag_squared():
    p = lax.broadcasted_iota(jnp.int32, (2 * TILE, TILE), 0)
    j = lax.broadcasted_iota(jnp.int32, (2 * TILE, TILE), 1)
    lag = (p - j - MAXREACH).astype(F32)
    return lag * lag


def zonal_rows(hi_ref, lo_ref, out_ref, params_ref, first_row, blocks):
    t2 = lag_squared()
    channels = hi_ref.shape[0] // GROUP
    for r in range(GROUP):
        row = first_row + r
        coef, shift, limit = params_ref[0, row], params_ref[1, row], params_ref[2, row]
        band = jnp.where(t2 <= limit, jnp.exp2(t2 * coef + shift), 0.0)
        band = jnp.concatenate(split(band), axis=1)
        rows = slice(r * channels, (r + 1) * channels)
        parts = []
        for ref in (hi_ref, lo_ref):
            for b in range(blocks):
                parts.append(ref[rows, b * TILE:(b + 2) * TILE])
        prod = dot(jnp.concatenate(parts, axis=0), band)
        n = blocks * channels
        total = prod[:n, :TILE] + (prod[:n, TILE:] + prod[n:, :TILE])
        for b in range(blocks):
            out_ref[rows, b * TILE:(b + 1) * TILE] = total[b * channels:(b + 1) * channels]


MESH = pl.DeviceIdType.MESH


def build_kron(mixing_ref, fwd_hi, fwd_lo, adj_hi, adj_lo):
    channels = mixing_ref.shape[0]
    size = channels * GROUP

    def grid(dim, of):
        index = lax.broadcasted_iota(jnp.int32, (size, size), dim)
        return index % of, index // of

    def spread(matrix, row_fast, col_fast):
        rest = matrix
        rows = lax.broadcasted_iota(jnp.int32, (size, channels), 0)
        rows = rows % channels if row_fast else rows // GROUP
        cols = lax.broadcasted_iota(jnp.int32, (channels, size), 1)
        cols = cols % channels if col_fast else cols // GROUP
        pick_rows = rows == lax.broadcasted_iota(jnp.int32, (size, channels), 1)
        pick_cols = cols == lax.broadcasted_iota(jnp.int32, (channels, size), 0)
        pick_rows = jnp.where(pick_rows, 1.0, 0.0).astype(BF)
        pick_cols = jnp.where(pick_cols, 1.0, 0.0).astype(BF)
        total = jnp.zeros((size, size), F32)
        for _ in range(3):
            part = rest.astype(BF)
            rest = rest - part.astype(F32)
            total = total + dot(dot(pick_rows, part).astype(BF), pick_cols)
        return total

    mixing = mixing_ref[...]
    for hi_ref, lo_ref, mix, a, p in (
        (fwd_hi, fwd_lo, spread(mixing, True, False), grid(0, channels)[1], grid(1, GROUP)[0]),
        (adj_hi, adj_lo, spread(mixing.T, False, True), grid(0, GROUP)[0], grid(1, channels)[1]),
    ):
        for half in range(2):
            hi, lo = split(merid_weights((p - a + (half * GROUP - MREACH)).astype(F32)) * mix)
            hi_ref[half] = hi
            lo_ref[half] = lo


def route_kernel(
    n_lat, n_lon, cols, owner_ref, cell_ref, chan_ref, weight_ref, out_ref,
    sent, got, send_sem, recv_sem,
):
    devices = n_lat * n_lon
    me = lax.axis_index("lat") * n_lon + lax.axis_index("lon")

    def device(k):
        peer = lax.rem(me + k, devices)
        return peer // n_lon, lax.rem(peer, n_lon)

    barrier = pltpu.get_barrier_semaphore()

    def greet(k, _):
        pl.semaphore_signal(barrier, inc=1, device_id=device(k), device_id_type=MESH)
        return 0

    lax.fori_loop(1, devices, greet, 0)
    count = owner_ref.shape[1]
    chunk = math.gcd(count, 256)
    hits = lax.broadcasted_iota(jnp.int32, (devices, count), 0) == owner_ref[...]
    hits_f = jnp.where(hits, 1.0, 0.0)
    hits_b = hits_f.astype(BF)
    upper = (
        lax.broadcasted_iota(jnp.int32, (chunk, chunk), 0)
        < lax.broadcasted_iota(jnp.int32, (chunk, chunk), 1)
    )
    upper = jnp.where(upper, 1.0, 0.0).astype(BF)
    base = jnp.zeros((devices, 1), F32)
    ranks = []
    for k in range(count // chunk):
        part = slice(k * chunk, (k + 1) * chunk)
        before = dot(hits_b[:, part], upper) + base
        ranks.append(jnp.sum(before * hits_f[:, part], axis=0, keepdims=True))
        base = base + jnp.sum(hits_f[:, part], axis=1, keepdims=True)
    rank = jnp.concatenate(ranks, axis=1).astype(jnp.int32)
    rank_hits = lax.broadcasted_iota(jnp.int32, (CAP, count), 0) == rank
    flat = cell_ref[...] + chan_ref[...]
    digits = [flat & 127, (flat >> 7) & 127, flat >> 14]
    pieces = [weight_ref[...].astype(F32)] + [d.astype(F32) for d in digits]
    table = jnp.concatenate([jnp.where(rank_hits, v, 0.0) for v in pieces], axis=0).astype(BF)
    out = lax.dot_general(hits_b, table, (((1,), (1,)), ((), ())), preferred_element_type=F32)
    place = (
        out[:, CAP:2 * CAP] + 128.0 * out[:, 2 * CAP:3 * CAP] + 16384.0 * out[:, 3 * CAP:]
    )
    packed = jnp.concatenate([out[:, :CAP], place], axis=1)
    for d in range(devices):
        sent[d] = packed[d:d + 1]
    pl.semaphore_wait(barrier, devices - 1)

    def copy(k):
        return pltpu.make_async_remote_copy(
            src_ref=sent.at[lax.rem(me + k, devices)],
            dst_ref=got.at[k],
            send_sem=send_sem.at[k],
            recv_sem=recv_sem.at[k],
            device_id=device(k),
            device_id_type=MESH,
        )

    def start(k, _):
        copy(k).start()
        return 0

    def finish(k, _):
        copy(k).wait()
        return 0

    lax.fori_loop(1, devices, start, 0)
    got[0] = sent[me]
    lax.fori_loop(1, devices, finish, 0)
    for k in range(devices // 2):
        first, second = got[2 * k], got[2 * k + 1]
        lanes = slice(2 * CAP * k, 2 * CAP * (k + 1))
        out_ref[0:1, lanes] = jnp.concatenate([first[:, :CAP], second[:, :CAP]], axis=1)
        out_ref[1:2, lanes] = jnp.concatenate([first[:, CAP:], second[:, CAP:]], axis=1)


DIRS = ((-1, 0), (1, 0), (0, -1), (0, 1), (-1, -1), (-1, 1), (1, -1), (1, 1))


def main_kernel(
    n_lat, n_lon, params_ref, got_ref, mixing_ref, control_ref, sigma_ref, inc_ref, grad_ref,
    tall, sigma, inc, grad, ext, colhot, hi_ref, lo_ref, zon_ref, fhi_ref, flo_ref, fzon_ref, carry,
    kron_fh, kron_fl, kron_ah, kron_al,
    rows_in, halo_out, halo_in, edge_in, side_out, side_in, corner_out, corner_in,
    load_sem, store_sem, fsend, frecv, asend, arecv,
):
    channels, rows, cols = control_ref.shape
    received = got_ref.shape[1]
    lines = channels * GROUP
    wide = cols + TILE
    tall_rows = rows + 2 * MREACH
    groups = rows // GROUP
    chunk = math.gcd(received, 2048)
    half_tall, half_rows = tall_rows // 2, rows // 2
    lat, lon = lax.axis_index("lat"), lax.axis_index("lon")

    def there(dlat, dlon):
        return lat + dlat, lax.rem(lon + dlon + n_lon, n_lon)

    def has(dlat):
        return (lat + dlat >= 0) & (lat + dlat < n_lat)

    def when(dlat, action):
        if dlat == 0:
            action()
        else:
            pl.when(has(dlat))(action)

    barrier = pltpu.get_barrier_semaphore()
    for dlat, dlon in DIRS:
        when(dlat, lambda dlat=dlat, dlon=dlon: pl.semaphore_signal(
            barrier, inc=1, device_id=there(dlat, dlon), device_id_type=MESH))
    load_control = pltpu.make_async_copy(
        control_ref, tall.at[:, pl.ds(MREACH, rows), :], load_sem.at[0])
    load_sigma = pltpu.make_async_copy(sigma_ref, sigma, load_sem.at[1])
    load_control.start()
    load_sigma.start()
    sides = jnp.where(lat > 0, 1, 0) + jnp.where(lat < n_lat - 1, 1, 0)
    pl.semaphore_wait(barrier, 2 + 3 * sides)

    def remote(src, dst, sems, index, dlat, dlon):
        return pltpu.make_async_remote_copy(
            src_ref=src, dst_ref=dst, send_sem=sems[0].at[index], recv_sem=sems[1].at[index],
            device_id=there(dlat, dlon), device_id_type=MESH)

    row_copies = [
        remote(control_ref.at[:, pl.ds(0, MREACH), :], rows_in.at[0], (fsend, frecv), 0, -1, 0),
        remote(control_ref.at[:, pl.ds(rows - MREACH, MREACH), :], rows_in.at[1],
               (fsend, frecv), 1, 1, 0),
    ]
    halo_copies = [
        remote(halo_out.at[0], halo_in.at[0], (fsend, frecv), 2, 0, -1),
        remote(halo_out.at[1], halo_in.at[1], (fsend, frecv), 3, 0, 1),
    ]
    when(-1, row_copies[0].start)
    when(1, row_copies[1].start)

    def place(k):
        flat = got_ref[1:2, pl.ds(k * chunk, chunk)].astype(jnp.int32)
        return got_ref[0:1, pl.ds(k * chunk, chunk)], flat

    build_kron(mixing_ref, kron_fh, kron_fl, kron_ah, kron_al)
    carry[...] = jnp.zeros_like(carry)
    hi_ref[...] = jnp.zeros_like(hi_ref)
    lo_ref[...] = jnp.zeros_like(lo_ref)
    for k in range(received // chunk):
        col = place(k)[1] % cols
        hot = lax.broadcasted_iota(jnp.int32, (cols, chunk), 0) == col
        colhot[:, k * chunk:(k + 1) * chunk] = jnp.where(hot, 1.0, 0.0).astype(BF)
    load_sigma.wait()

    def send_halo():
        load_control.wait()
        for index, dlat, start in ((0, -1, rows + MREACH), (1, 1, 0)):
            when(dlat, row_copies[index].wait_send)

            @pl.when(has(-dlat))
            def _():
                row_copies[index].wait_recv()
                tall[:, start:start + MREACH, :] = rows_in[index]

            @pl.when(jnp.logical_not(has(-dlat)))
            def _():
                tall[:, start:start + MREACH, :] = jnp.zeros((channels, MREACH, cols), F32)
        for index, lanes in ((0, slice(0, MAXREACH)), (1, slice(TILE - MAXREACH, TILE))):
            tile = slice(0, TILE) if index == 0 else slice(cols - TILE, cols)
            top = tall[:, :half_tall, tile][:, :, lanes]
            bottom = tall[:, half_tall:, tile][:, :, lanes]
            halo_out[index] = jnp.concatenate([top, bottom], axis=2)
        for copy in halo_copies:
            copy.start()

    def adjoint_group(g, _):
        pl.when(g == 1)(send_halo)
        place_ids = lax.broadcasted_iota(jnp.int32, (lines, chunk), 0)
        total = jnp.zeros((lines, cols), F32)
        for k in range(received // chunk):
            value, flat = place(k)
            line = flat // cols
            chan, row = line // rows, line % rows - g * GROUP
            inside = (row >= 0) & (row < GROUP)
            target = jnp.where(inside, chan * GROUP + row, -1)
            rowhot = jnp.where(place_ids == target, value, 0.0).astype(BF)
            total = total + lax.dot_general(
                rowhot, colhot[:, k * chunk:(k + 1) * chunk],
                (((1,), (1,)), ((), ())), preferred_element_type=F32,
            )
        here = pl.ds(pl.multiple_of(g * GROUP, GROUP), GROUP)
        weighted = total.reshape(channels, GROUP, cols) * sigma[:, here, :]
        hi, lo = split(jnp.swapaxes(weighted, 0, 1).reshape(lines, cols))
        hi_ref[:, TILE:TILE + cols] = hi
        lo_ref[:, TILE:TILE + cols] = lo
        zonal_rows(hi_ref, lo_ref, zon_ref, params_ref, g * GROUP, wide // TILE)
        z_hi, z_lo = split(zon_ref[...])
        done = carry[...] + (
            dot(kron_ah[1], z_hi) + (dot(kron_ah[1], z_lo) + dot(kron_al[1], z_hi))
        )
        ext[:, here, :] = done.reshape(channels, GROUP, wide)
        carry[...] = dot(kron_ah[0], z_hi) + (dot(kron_ah[0], z_lo) + dot(kron_al[0], z_hi))
        return 0

    lax.fori_loop(0, groups, adjoint_group, 0)
    ext[:, rows:rows + GROUP, :] = carry[...].reshape(channels, GROUP, wide)

    for index, tile in ((0, slice(0, TILE)), (1, slice(wide - TILE, wide))):
        lanes = slice(0, MAXREACH) if index == 0 else slice(TILE - MAXREACH, TILE)
        top = ext[:, MREACH:MREACH + half_rows, tile][:, :, lanes]
        bottom = ext[:, MREACH + half_rows:MREACH + rows, tile][:, :, lanes]
        side_out[index] = jnp.concatenate([top, bottom], axis=2)
        corner_out[index] = ext[:, :MREACH, tile]
        corner_out[2 + index] = ext[:, rows + MREACH:, tile]
    sems = (asend, arecv)
    fringe = [
        remote(ext.at[:, pl.ds(0, MREACH), :], edge_in.at[0], sems, 0, -1, 0),
        remote(ext.at[:, pl.ds(rows + MREACH, MREACH), :], edge_in.at[1], sems, 1, 1, 0),
        remote(side_out.at[0], side_in.at[0], sems, 2, 0, -1),
        remote(side_out.at[1], side_in.at[1], sems, 3, 0, 1),
    ] + [
        remote(corner_out.at[i], corner_in.at[i], sems, 4 + i, *DIRS[4 + i]) for i in range(4)
    ]
    for (dlat, _), copy in zip(DIRS, fringe):
        when(dlat, copy.start)

    for copy in halo_copies:
        copy.wait()

    def forward_group(e, _):
        here = pl.ds(pl.multiple_of(e * GROUP, GROUP), GROUP)
        body = tall[:, here, :]

        def column(packed_ref):
            pieces = []
            for part in range(GROUP // 8):
                first = e * GROUP + part * 8
                second = first >= half_tall
                line = pl.multiple_of(jnp.where(second, first - half_tall, first), 8)
                both = packed_ref[:, pl.ds(line, 8), :]
                pieces.append(jnp.where(second, both[:, :, MAXREACH:], both[:, :, :MAXREACH]))
            return jnp.concatenate(pieces, axis=1)

        block = jnp.concatenate([column(halo_in.at[1]), body, column(halo_in.at[0])], axis=2)
        e_hi, e_lo = split(block.reshape(lines, wide))

        @pl.when(e > 0)
        def _():
            total = carry[...] + (
                dot(kron_fh[1], e_hi) + (dot(kron_fh[1], e_lo) + dot(kron_fl[1], e_hi))
            )
            hi, lo = split(total)
            fhi_ref[...] = hi
            flo_ref[...] = lo
            first = (e - 1) * GROUP
            zonal_rows(fhi_ref, flo_ref, fzon_ref, params_ref, first, cols // TILE)
            smooth = jnp.swapaxes(fzon_ref[...].reshape(GROUP, channels, cols), 0, 1)
            there_rows = pl.ds(pl.multiple_of(first, GROUP), GROUP)
            inc[:, there_rows, :] = smooth * sigma[:, there_rows, :]
        carry[...] = dot(kron_fh[0], e_hi) + (dot(kron_fh[0], e_lo) + dot(kron_fl[0], e_hi))
        return 0

    lax.fori_loop(0, groups + 1, forward_group, 0)
    store_inc = pltpu.make_async_copy(inc, inc_ref, store_sem.at[0])
    store_inc.start()

    grad[...] = ext[:, MREACH:MREACH + rows, MAXREACH:MAXREACH + cols]
    first_tile, last_tile = slice(0, TILE), slice(cols - TILE, cols)
    for (dlat, _), copy in zip(DIRS, fringe):
        when(dlat, copy.wait_send)
        when(-dlat, copy.wait_recv)
    zero = jnp.zeros((channels, half_rows, MAXREACH), F32)
    for part in range(2):
        lanes = slice(part * MAXREACH, (part + 1) * MAXREACH)
        span = slice(part * half_rows, (part + 1) * half_rows)
        grad[:, span, last_tile] += jnp.concatenate([zero, side_in[0][:, :, lanes]], axis=2)
        grad[:, span, first_tile] += jnp.concatenate([side_in[1][:, :, lanes], zero], axis=2)
    small = jnp.zeros((channels, MREACH, MAXREACH), F32)
    for index, dlat, span in ((0, -1, slice(rows - MREACH, rows)), (1, 1, slice(0, MREACH))):
        @pl.when(has(-dlat))
        def _():
            grad[:, span, :] += edge_in[index][:, :, MAXREACH:MAXREACH + cols]
            right, left = corner_in[2 * index], corner_in[2 * index + 1]
            grad[:, span, last_tile] += jnp.concatenate([small, right[:, :, :MAXREACH]], axis=2)
            grad[:, span, first_tile] += jnp.concatenate([left[:, :, MAXREACH:], small], axis=2)
    store_grad = pltpu.make_async_copy(grad, grad_ref, store_sem.at[1])
    store_grad.start()
    store_inc.wait()
    store_grad.wait()


def local(
    n_lat, n_lon, control, sigma_field, mixing, zonal_reach, obs_owner, obs_cell, obs_chan, obs_weight
):
    channels, rows, cols = control.shape
    devices = n_lat * n_lon
    received = devices * CAP
    lines, wide = channels * GROUP, cols + TILE
    count = obs_cell.shape[0]
    smem = pl.BlockSpec(memory_space=pltpu.SMEM)
    vmem = pl.BlockSpec(memory_space=pltpu.VMEM)
    anywhere = pl.BlockSpec(memory_space=pl.ANY)
    got = pl.pallas_call(
        lambda *refs: route_kernel(n_lat, n_lon, cols, *refs),
        out_shape=jax.ShapeDtypeStruct((2, received), F32),
        in_specs=[vmem] * 4,
        out_specs=vmem,
        scratch_shapes=[
            pltpu.VMEM((devices, 1, 2 * CAP), F32),
            pltpu.VMEM((devices, 1, 2 * CAP), F32),
            pltpu.SemaphoreType.DMA((devices,)),
            pltpu.SemaphoreType.DMA((devices,)),
        ],
        compiler_params=pltpu.CompilerParams(
            vmem_limit_bytes=32 * 2**20, collective_id=0, has_side_effects=True
        ),
        name="route",
    )(
        obs_owner.reshape(1, count),
        obs_cell.reshape(1, count),
        (obs_chan * (rows * cols)).reshape(1, count),
        obs_weight.reshape(1, count),
    )
    tall_rows = rows + 2 * MREACH
    halo = pltpu.VMEM((2, channels, tall_rows // 2, TILE), F32)
    side = pltpu.VMEM((2, channels, rows // 2, TILE), F32)
    corner = pltpu.VMEM((4, channels, MREACH, TILE), F32)
    kron = pltpu.VMEM((2, lines, lines), BF)
    out = jax.ShapeDtypeStruct((channels, rows, cols), F32)
    return pl.pallas_call(
        lambda *refs: main_kernel(n_lat, n_lon, *refs),
        out_shape=(out, out),
        in_specs=[smem, vmem, vmem, anywhere, anywhere],
        out_specs=(anywhere, anywhere),
        scratch_shapes=[
            pltpu.VMEM((channels, tall_rows, cols), F32),
            pltpu.VMEM((channels, rows, cols), F32),
            pltpu.VMEM((channels, rows, cols), F32),
            pltpu.VMEM((channels, rows, cols), F32),
            pltpu.VMEM((channels, tall_rows, wide), F32),
            pltpu.VMEM((cols, received), BF),
            pltpu.VMEM((lines, wide + TILE), BF),
            pltpu.VMEM((lines, wide + TILE), BF),
            pltpu.VMEM((lines, wide), F32),
            pltpu.VMEM((lines, wide), BF),
            pltpu.VMEM((lines, wide), BF),
            pltpu.VMEM((lines, cols), F32),
            pltpu.VMEM((lines, wide), F32),
            kron, kron, kron, kron,
            pltpu.VMEM((2, channels, MREACH, cols), F32),
            halo, halo,
            pltpu.VMEM((2, channels, MREACH, wide), F32),
            side, side, corner, corner,
            pltpu.SemaphoreType.DMA((2,)),
            pltpu.SemaphoreType.DMA((2,)),
            pltpu.SemaphoreType.DMA((4,)),
            pltpu.SemaphoreType.DMA((4,)),
            pltpu.SemaphoreType.DMA((8,)),
            pltpu.SemaphoreType.DMA((8,)),
        ],
        compiler_params=pltpu.CompilerParams(
            vmem_limit_bytes=60 * 2**20, collective_id=1, has_side_effects=True
        ),
        name="main",
    )(row_params(zonal_reach), got, mixing, control, sigma_field)


def solution(mesh):
    return jax.shard_map(
        functools.partial(local, mesh.shape["lat"], mesh.shape["lon"]),
        mesh=mesh,
        in_specs=(
            P(None, "lat", "lon"),
            P(None, "lat", "lon"),
            P(),
            P("lat"),
            P(("lat", "lon"), None),
            P(("lat", "lon")),
            P(("lat", "lon")),
            P(("lat", "lon")),
        ),
        out_specs=(P(None, "lat", "lon"), P(None, "lat", "lon")),
        check_vma=False,
    )
```

```python
import functools
import math

import jax
import jax.numpy as jnp
from jax import lax
from jax.experimental import pallas as pl
from jax.experimental.pallas import tpu as pltpu
from jax.sharding import PartitionSpec as P

CAP = 64
MAXREACH = 64
MREACH = 8
GROUP = 16
TILE = 128
BF = jnp.bfloat16
F32 = jnp.float32
LOG2E = math.log2(math.e)


def merid_weights(lag):
    taps = [math.exp(-0.5 * (3.0 * t / MREACH) ** 2) for t in range(-MREACH, MREACH + 1)]
    norm = math.sqrt(sum(w * w for w in taps))
    scaled = lag * (3.0 / MREACH)
    return jnp.where(jnp.abs(lag) <= MREACH, jnp.exp(-0.5 * scaled * scaled) / norm, 0.0)


def split(x):
    hi = x.astype(BF)
    return hi, (x - hi.astype(F32)).astype(BF)


def dot(a, b):
    return jnp.dot(a, b, preferred_element_type=F32)


def lag_squared():
    p = lax.broadcasted_iota(jnp.int32, (2 * TILE, TILE), 0)
    j = lax.broadcasted_iota(jnp.int32, (2 * TILE, TILE), 1)
    lag = (p - j - MAXREACH).astype(F32)
    return lag * lag


def zonal_rows(hi_ref, lo_ref, out_ref, reach_ref, first_row, blocks):
    t2 = lag_squared()
    side2 = (lax.broadcasted_iota(jnp.int32, (1, TILE), 1) + 1).astype(F32)
    side2 = side2 * side2
    channels = hi_ref.shape[0] // GROUP
    for r in range(GROUP):
        row = first_row + r
        reach = reach_ref[row].astype(F32)
        limit = jnp.full((1, TILE), reach * reach)
        coef = (-4.5 * LOG2E) / limit
        side = jnp.where(side2 <= limit, jnp.exp2(side2 * coef), 0.0)
        norm = 2.0 * jnp.sum(side * side, axis=1, keepdims=True) + 1.0
        shift = -0.5 * jnp.log2(norm)
        band = jnp.where(t2 <= limit, jnp.exp2(t2 * coef + shift), 0.0)
        band = jnp.concatenate(split(band), axis=1)
        rows = slice(r * channels, (r + 1) * channels)
        parts = []
        for ref in (hi_ref, lo_ref):
            for b in range(blocks):
                parts.append(ref[rows, b * TILE:(b + 2) * TILE])
        prod = dot(jnp.concatenate(parts, axis=0), band)
        n = blocks * channels
        total = prod[:n, :TILE] + (prod[:n, TILE:] + prod[n:, :TILE])
        for b in range(blocks):
            out_ref[rows, b * TILE:(b + 1) * TILE] = total[b * channels:(b + 1) * channels]


MESH = pl.DeviceIdType.MESH


def build_kron(mixing_ref, fwd_hi, fwd_lo, adj_hi, adj_lo):
    channels = mixing_ref.shape[0]
    size = channels * GROUP

    def grid(dim, of):
        index = lax.broadcasted_iota(jnp.int32, (size, size), dim)
        return index % of, index // of

    def spread(matrix, row_fast, col_fast):
        rest = matrix
        rows = lax.broadcasted_iota(jnp.int32, (size, channels), 0)
        rows = rows % channels if row_fast else rows // GROUP
        cols = lax.broadcasted_iota(jnp.int32, (channels, size), 1)
        cols = cols % channels if col_fast else cols // GROUP
        pick_rows = rows == lax.broadcasted_iota(jnp.int32, (size, channels), 1)
        pick_cols = cols == lax.broadcasted_iota(jnp.int32, (channels, size), 0)
        pick_rows = jnp.where(pick_rows, 1.0, 0.0).astype(BF)
        pick_cols = jnp.where(pick_cols, 1.0, 0.0).astype(BF)
        total = jnp.zeros((size, size), F32)
        for _ in range(3):
            part = rest.astype(BF)
            rest = rest - part.astype(F32)
            total = total + dot(dot(pick_rows, part).astype(BF), pick_cols)
        return total

    mixing = mixing_ref[...]
    for hi_ref, lo_ref, mix, a, p in (
        (fwd_hi, fwd_lo, spread(mixing, True, False), grid(0, channels)[1], grid(1, GROUP)[0]),
        (adj_hi, adj_lo, spread(mixing.T, False, True), grid(0, GROUP)[0], grid(1, channels)[1]),
    ):
        for half in range(2):
            hi, lo = split(merid_weights((p - a + (half * GROUP - MREACH)).astype(F32)) * mix)
            hi_ref[half] = hi
            lo_ref[half] = lo


def route_kernel(
    n_lat, n_lon, cols, owner_ref, cell_ref, chan_ref, weight_ref, out_ref,
    sent, got, send_sem, recv_sem,
):
    devices = n_lat * n_lon
    me = lax.axis_index("lat") * n_lon + lax.axis_index("lon")

    def device(k):
        peer = lax.rem(me + k, devices)
        return peer // n_lon, lax.rem(peer, n_lon)

    barrier = pltpu.get_barrier_semaphore()

    def greet(k, _):
        pl.semaphore_signal(barrier, inc=1, device_id=device(k), device_id_type=MESH)
        return 0

    lax.fori_loop(1, devices, greet, 0)
    count = owner_ref.shape[1]
    chunk = math.gcd(count, 256)
    hits = lax.broadcasted_iota(jnp.int32, (devices, count), 0) == owner_ref[...]
    hits_f = jnp.where(hits, 1.0, 0.0)
    hits_b = hits_f.astype(BF)
    upper = (
        lax.broadcasted_iota(jnp.int32, (chunk, chunk), 0)
        < lax.broadcasted_iota(jnp.int32, (chunk, chunk), 1)
    )
    upper = jnp.where(upper, 1.0, 0.0).astype(BF)
    base = jnp.zeros((devices, 1), F32)
    ranks = []
    for k in range(count // chunk):
        part = slice(k * chunk, (k + 1) * chunk)
        before = dot(hits_b[:, part], upper) + base
        ranks.append(jnp.sum(before * hits_f[:, part], axis=0, keepdims=True))
        base = base + jnp.sum(hits_f[:, part], axis=1, keepdims=True)
    rank = jnp.concatenate(ranks, axis=1).astype(jnp.int32)
    rank_hits = lax.broadcasted_iota(jnp.int32, (CAP, count), 0) == rank
    flat = cell_ref[...] + chan_ref[...]
    digits = [flat & 127, (flat >> 7) & 127, flat >> 14]
    pieces = [weight_ref[...].astype(F32)] + [d.astype(F32) for d in digits]
    table = jnp.concatenate([jnp.where(rank_hits, v, 0.0) for v in pieces], axis=0).astype(BF)
    out = lax.dot_general(hits_b, table, (((1,), (1,)), ((), ())), preferred_element_type=F32)
    place = (
        out[:, CAP:2 * CAP] + 128.0 * out[:, 2 * CAP:3 * CAP] + 16384.0 * out[:, 3 * CAP:]
    )
    packed = jnp.concatenate([out[:, :CAP], place], axis=1)
    for d in range(devices):
        sent[d] = packed[d:d + 1]
    pl.semaphore_wait(barrier, devices - 1)

    def copy(k):
        return pltpu.make_async_remote_copy(
            src_ref=sent.at[lax.rem(me + k, devices)],
            dst_ref=got.at[k],
            send_sem=send_sem.at[k],
            recv_sem=recv_sem.at[k],
            device_id=device(k),
            device_id_type=MESH,
        )

    def start(k, _):
        copy(k).start()
        return 0

    def finish(k, _):
        copy(k).wait()
        return 0

    lax.fori_loop(1, devices, start, 0)
    got[0] = sent[me]
    lax.fori_loop(1, devices, finish, 0)
    for k in range(devices // 2):
        first, second = got[2 * k], got[2 * k + 1]
        lanes = slice(2 * CAP * k, 2 * CAP * (k + 1))
        out_ref[0:1, lanes] = jnp.concatenate([first[:, :CAP], second[:, :CAP]], axis=1)
        out_ref[1:2, lanes] = jnp.concatenate([first[:, CAP:], second[:, CAP:]], axis=1)


DIRS = ((-1, 0), (1, 0), (0, -1), (0, 1), (-1, -1), (-1, 1), (1, -1), (1, 1))


def main_kernel(
    n_lat, n_lon, reach_ref, got_ref, mixing_ref, control_ref, sigma_ref, inc_ref, grad_ref,
    tall, sigma, inc, grad, ext, colhot, hi_ref, lo_ref, zon_ref, fhi_ref, flo_ref, fzon_ref, carry,
    kron_fh, kron_fl, kron_ah, kron_al,
    rows_in, halo_out, halo_in, edge_in, side_out, side_in, corner_out, corner_in,
    load_sem, store_sem, fsend, frecv, asend, arecv,
):
    channels, rows, cols = control_ref.shape
    received = got_ref.shape[1]
    lines = channels * GROUP
    wide = cols + TILE
    tall_rows = rows + 2 * MREACH
    groups = rows // GROUP
    chunk = math.gcd(received, 2048)
    half_tall, half_rows = tall_rows // 2, rows // 2
    lat, lon = lax.axis_index("lat"), lax.axis_index("lon")

    def there(dlat, dlon):
        return lat + dlat, lax.rem(lon + dlon + n_lon, n_lon)

    def has(dlat):
        return (lat + dlat >= 0) & (lat + dlat < n_lat)

    def when(dlat, action):
        if dlat == 0:
            action()
        else:
            pl.when(has(dlat))(action)

    barrier = pltpu.get_barrier_semaphore()
    for dlat, dlon in DIRS:
        when(dlat, lambda dlat=dlat, dlon=dlon: pl.semaphore_signal(
            barrier, inc=1, device_id=there(dlat, dlon), device_id_type=MESH))
    load_control = pltpu.make_async_copy(
        control_ref, tall.at[:, pl.ds(MREACH, rows), :], load_sem.at[0])
    load_sigma = pltpu.make_async_copy(sigma_ref, sigma, load_sem.at[1])
    load_control.start()
    load_sigma.start()
    sides = jnp.where(lat > 0, 1, 0) + jnp.where(lat < n_lat - 1, 1, 0)
    pl.semaphore_wait(barrier, 2 + 3 * sides)

    def remote(src, dst, sems, index, dlat, dlon):
        return pltpu.make_async_remote_copy(
            src_ref=src, dst_ref=dst, send_sem=sems[0].at[index], recv_sem=sems[1].at[index],
            device_id=there(dlat, dlon), device_id_type=MESH)

    row_copies = [
        remote(control_ref.at[:, pl.ds(0, MREACH), :], rows_in.at[0], (fsend, frecv), 0, -1, 0),
        remote(control_ref.at[:, pl.ds(rows - MREACH, MREACH), :], rows_in.at[1],
               (fsend, frecv), 1, 1, 0),
    ]
    halo_copies = [
        remote(halo_out.at[0], halo_in.at[0], (fsend, frecv), 2, 0, -1),
        remote(halo_out.at[1], halo_in.at[1], (fsend, frecv), 3, 0, 1),
    ]
    when(-1, row_copies[0].start)
    when(1, row_copies[1].start)

    def place(k):
        flat = got_ref[1:2, pl.ds(k * chunk, chunk)].astype(jnp.int32)
        return got_ref[0:1, pl.ds(k * chunk, chunk)], flat

    build_kron(mixing_ref, kron_fh, kron_fl, kron_ah, kron_al)
    carry[...] = jnp.zeros_like(carry)
    hi_ref[...] = jnp.zeros_like(hi_ref)
    lo_ref[...] = jnp.zeros_like(lo_ref)
    for k in range(received // chunk):
        col = place(k)[1] % cols
        hot = lax.broadcasted_iota(jnp.int32, (cols, chunk), 0) == col
        colhot[:, k * chunk:(k + 1) * chunk] = jnp.where(hot, 1.0, 0.0).astype(BF)
    load_sigma.wait()

    def send_halo():
        load_control.wait()
        for index, dlat, start in ((0, -1, rows + MREACH), (1, 1, 0)):
            when(dlat, row_copies[index].wait_send)

            @pl.when(has(-dlat))
            def _():
                row_copies[index].wait_recv()
                tall[:, start:start + MREACH, :] = rows_in[index]

            @pl.when(jnp.logical_not(has(-dlat)))
            def _():
                tall[:, start:start + MREACH, :] = jnp.zeros((channels, MREACH, cols), F32)
        for index, lanes in ((0, slice(0, MAXREACH)), (1, slice(TILE - MAXREACH, TILE))):
            tile = slice(0, TILE) if index == 0 else slice(cols - TILE, cols)
            top = tall[:, :half_tall, tile][:, :, lanes]
            bottom = tall[:, half_tall:, tile][:, :, lanes]
            halo_out[index] = jnp.concatenate([top, bottom], axis=2)
        for copy in halo_copies:
            copy.start()

    def adjoint_group(g, _):
        pl.when(g == 1)(send_halo)
        place_ids = lax.broadcasted_iota(jnp.int32, (lines, chunk), 0)
        total = jnp.zeros((lines, cols), F32)
        for k in range(received // chunk):
            value, flat = place(k)
            line = flat // cols
            chan, row = line // rows, line % rows - g * GROUP
            inside = (row >= 0) & (row < GROUP)
            target = jnp.where(inside, chan * GROUP + row, -1)
            rowhot = jnp.where(place_ids == target, value, 0.0).astype(BF)
            total = total + lax.dot_general(
                rowhot, colhot[:, k * chunk:(k + 1) * chunk],
                (((1,), (1,)), ((), ())), preferred_element_type=F32,
            )
        here = pl.ds(pl.multiple_of(g * GROUP, GROUP), GROUP)
        weighted = total.reshape(channels, GROUP, cols) * sigma[:, here, :]
        hi, lo = split(jnp.swapaxes(weighted, 0, 1).reshape(lines, cols))
        hi_ref[:, TILE:TILE + cols] = hi
        lo_ref[:, TILE:TILE + cols] = lo
        zonal_rows(hi_ref, lo_ref, zon_ref, reach_ref, g * GROUP, wide // TILE)
        z_hi, z_lo = split(zon_ref[...])
        done = carry[...] + (
            dot(kron_ah[1], z_hi) + (dot(kron_ah[1], z_lo) + dot(kron_al[1], z_hi))
        )
        ext[:, here, :] = done.reshape(channels, GROUP, wide)
        carry[...] = dot(kron_ah[0], z_hi) + (dot(kron_ah[0], z_lo) + dot(kron_al[0], z_hi))
        return 0

    lax.fori_loop(0, groups, adjoint_group, 0)
    ext[:, rows:rows + GROUP, :] = carry[...].reshape(channels, GROUP, wide)

    for index, tile in ((0, slice(0, TILE)), (1, slice(wide - TILE, wide))):
        lanes = slice(0, MAXREACH) if index == 0 else slice(TILE - MAXREACH, TILE)
        top = ext[:, MREACH:MREACH + half_rows, tile][:, :, lanes]
        bottom = ext[:, MREACH + half_rows:MREACH + rows, tile][:, :, lanes]
        side_out[index] = jnp.concatenate([top, bottom], axis=2)
        corner_out[index] = ext[:, :MREACH, tile]
        corner_out[2 + index] = ext[:, rows + MREACH:, tile]
    sems = (asend, arecv)
    fringe = [
        remote(ext.at[:, pl.ds(0, MREACH), :], edge_in.at[0], sems, 0, -1, 0),
        remote(ext.at[:, pl.ds(rows + MREACH, MREACH), :], edge_in.at[1], sems, 1, 1, 0),
        remote(side_out.at[0], side_in.at[0], sems, 2, 0, -1),
        remote(side_out.at[1], side_in.at[1], sems, 3, 0, 1),
    ] + [
        remote(corner_out.at[i], corner_in.at[i], sems, 4 + i, *DIRS[4 + i]) for i in range(4)
    ]
    for (dlat, _), copy in zip(DIRS, fringe):
        when(dlat, copy.start)

    for copy in halo_copies:
        copy.wait()

    def forward_group(e, _):
        here = pl.ds(pl.multiple_of(e * GROUP, GROUP), GROUP)
        body = tall[:, here, :]

        def column(packed_ref):
            pieces = []
            for part in range(GROUP // 8):
                first = e * GROUP + part * 8
                second = first >= half_tall
                line = pl.multiple_of(jnp.where(second, first - half_tall, first), 8)
                both = packed_ref[:, pl.ds(line, 8), :]
                pieces.append(jnp.where(second, both[:, :, MAXREACH:], both[:, :, :MAXREACH]))
            return jnp.concatenate(pieces, axis=1)

        block = jnp.concatenate([column(halo_in.at[1]), body, column(halo_in.at[0])], axis=2)
        e_hi, e_lo = split(block.reshape(lines, wide))

        @pl.when(e > 0)
        def _():
            total = carry[...] + (
                dot(kron_fh[1], e_hi) + (dot(kron_fh[1], e_lo) + dot(kron_fl[1], e_hi))
            )
            hi, lo = split(total)
            fhi_ref[...] = hi
            flo_ref[...] = lo
            first = (e - 1) * GROUP
            zonal_rows(fhi_ref, flo_ref, fzon_ref, reach_ref, first, cols // TILE)
            smooth = jnp.swapaxes(fzon_ref[...].reshape(GROUP, channels, cols), 0, 1)
            there_rows = pl.ds(pl.multiple_of(first, GROUP), GROUP)
            inc[:, there_rows, :] = smooth * sigma[:, there_rows, :]
        carry[...] = dot(kron_fh[0], e_hi) + (dot(kron_fh[0], e_lo) + dot(kron_fl[0], e_hi))
        return 0

    lax.fori_loop(0, groups + 1, forward_group, 0)
    store_inc = pltpu.make_async_copy(inc, inc_ref, store_sem.at[0])
    store_inc.start()

    grad[...] = ext[:, MREACH:MREACH + rows, MAXREACH:MAXREACH + cols]
    first_tile, last_tile = slice(0, TILE), slice(cols - TILE, cols)
    for (dlat, _), copy in zip(DIRS, fringe):
        when(dlat, copy.wait_send)
        when(-dlat, copy.wait_recv)
    zero = jnp.zeros((channels, half_rows, MAXREACH), F32)
    for part in range(2):
        lanes = slice(part * MAXREACH, (part + 1) * MAXREACH)
        span = slice(part * half_rows, (part + 1) * half_rows)
        grad[:, span, last_tile] += jnp.concatenate([zero, side_in[0][:, :, lanes]], axis=2)
        grad[:, span, first_tile] += jnp.concatenate([side_in[1][:, :, lanes], zero], axis=2)
    small = jnp.zeros((channels, MREACH, MAXREACH), F32)
    for index, dlat, span in ((0, -1, slice(rows - MREACH, rows)), (1, 1, slice(0, MREACH))):
        @pl.when(has(-dlat))
        def _():
            grad[:, span, :] += edge_in[index][:, :, MAXREACH:MAXREACH + cols]
            right, left = corner_in[2 * index], corner_in[2 * index + 1]
            grad[:, span, last_tile] += jnp.concatenate([small, right[:, :, :MAXREACH]], axis=2)
            grad[:, span, first_tile] += jnp.concatenate([left[:, :, MAXREACH:], small], axis=2)
    store_grad = pltpu.make_async_copy(grad, grad_ref, store_sem.at[1])
    store_grad.start()
    store_inc.wait()
    store_grad.wait()


def local(
    n_lat, n_lon, control, sigma_field, mixing, zonal_reach, obs_owner, obs_cell, obs_chan, obs_weight
):
    channels, rows, cols = control.shape
    devices = n_lat * n_lon
    received = devices * CAP
    lines, wide = channels * GROUP, cols + TILE
    count = obs_cell.shape[0]
    smem = pl.BlockSpec(memory_space=pltpu.SMEM)
    vmem = pl.BlockSpec(memory_space=pltpu.VMEM)
    anywhere = pl.BlockSpec(memory_space=pl.ANY)
    got = pl.pallas_call(
        lambda *refs: route_kernel(n_lat, n_lon, cols, *refs),
        out_shape=jax.ShapeDtypeStruct((2, received), F32),
        in_specs=[vmem] * 4,
        out_specs=vmem,
        scratch_shapes=[
            pltpu.VMEM((devices, 1, 2 * CAP), F32),
            pltpu.VMEM((devices, 1, 2 * CAP), F32),
            pltpu.SemaphoreType.DMA((devices,)),
            pltpu.SemaphoreType.DMA((devices,)),
        ],
        compiler_params=pltpu.CompilerParams(
            vmem_limit_bytes=32 * 2**20, collective_id=0, has_side_effects=True
        ),
        name="route",
    )(
        obs_owner.reshape(1, count),
        obs_cell.reshape(1, count),
        (obs_chan * (rows * cols)).reshape(1, count),
        obs_weight.reshape(1, count),
    )
    tall_rows = rows + 2 * MREACH
    halo = pltpu.VMEM((2, channels, tall_rows // 2, TILE), F32)
    side = pltpu.VMEM((2, channels, rows // 2, TILE), F32)
    corner = pltpu.VMEM((4, channels, MREACH, TILE), F32)
    kron = pltpu.VMEM((2, lines, lines), BF)
    out = jax.ShapeDtypeStruct((channels, rows, cols), F32)
    return pl.pallas_call(
        lambda *refs: main_kernel(n_lat, n_lon, *refs),
        out_shape=(out, out),
        in_specs=[smem, vmem, vmem, anywhere, anywhere],
        out_specs=(anywhere, anywhere),
        scratch_shapes=[
            pltpu.VMEM((channels, tall_rows, cols), F32),
            pltpu.VMEM((channels, rows, cols), F32),
            pltpu.VMEM((channels, rows, cols), F32),
            pltpu.VMEM((channels, rows, cols), F32),
            pltpu.VMEM((channels, tall_rows, wide), F32),
            pltpu.VMEM((cols, received), BF),
            pltpu.VMEM((lines, wide + TILE), BF),
            pltpu.VMEM((lines, wide + TILE), BF),
            pltpu.VMEM((lines, wide), F32),
            pltpu.VMEM((lines, wide), BF),
            pltpu.VMEM((lines, wide), BF),
            pltpu.VMEM((lines, cols), F32),
            pltpu.VMEM((lines, wide), F32),
            kron, kron, kron, kron,
            pltpu.VMEM((2, channels, MREACH, cols), F32),
            halo, halo,
            pltpu.VMEM((2, channels, MREACH, wide), F32),
            side, side, corner, corner,
            pltpu.SemaphoreType.DMA((2,)),
            pltpu.SemaphoreType.DMA((2,)),
            pltpu.SemaphoreType.DMA((4,)),
            pltpu.SemaphoreType.DMA((4,)),
            pltpu.SemaphoreType.DMA((8,)),
            pltpu.SemaphoreType.DMA((8,)),
        ],
        compiler_params=pltpu.CompilerParams(
            vmem_limit_bytes=42 * 2**20 + 2 * cols * received, collective_id=1, has_side_effects=True
        ),
        name="main",
    )(zonal_reach, got, mixing, control, sigma_field)


def solution(mesh):
    return jax.shard_map(
        functools.partial(local, mesh.shape["lat"], mesh.shape["lon"]),
        mesh=mesh,
        in_specs=(
            P(None, "lat", "lon"),
            P(None, "lat", "lon"),
            P(),
            P("lat"),
            P(("lat", "lon"), None),
            P(("lat", "lon")),
            P(("lat", "lon")),
            P(("lat", "lon")),
        ),
        out_specs=(P(None, "lat", "lon"), P(None, "lat", "lon")),
        check_vma=False,
    )
```
